512 devices in a mesh: dp: 8 (over y), pipe: 16 (over x, z_hi, core), tensor: 4 (over z_lo).
Axes of the slice: x: 4, y: 8, z: 8 (z_hi: 2, z_lo: 4; z = z_hi * 4 + z_lo), core: 2. Of those that a mesh axis runs over, the one named last changes fastest.
Arguments:
- final_normed: bfloat16 [16384, 7168], P(('dp', 'pipe'), 'tensor'), may hold values from -4 to 4
- embed_cot: bfloat16 [16384, 7168], P(('dp', 'pipe'), 'tensor'), may hold values from -1.796875 to 1.796875
- head: bfloat16 [512, 7168], P('tensor'), may hold values from -1 to 1
- rest_lse: float32 [16384], P(('dp', 'pipe')), may hold values from 6 to 12
- loss_grad: float32 [16384], P(('dp', 'pipe')), may hold values from 1 to 4
- target_ids: int32 [16384], P(('dp', 'pipe')), may hold values from 0 to 511
- embed_ids: int32 [16384], P(('dp', 'pipe')), may hold values from 0 to 63
Outputs:
- token_loss: float32 [16384], P(('dp', 'pipe'))
- grad_hidden: bfloat16 [16384, 7168], P(('dp', 'pipe'), 'tensor')
- head_grad: float32 [512, 7168], P('tensor', 'dp')
- embed_grad: float32 [64, 7168], P('dp', 'tensor')
The draws below stay inside these ranges and needn't reach their ends.
All inputs are finite; a program needn't handle non-finite values.
Results may differ from the reference program's by a relative error of at most 0.0047.
Values may be sent and summed in bfloat16 or wider, within the bound.
No kernel may reach another device: no remote copies, remote signals or barrier semaphores. Data moves between devices by JAX's collectives and lax.ppermute only.
A program may use at most 64 MiB of HBM per device.

```python
import math
import jax
import jax.numpy as jnp
import numpy as np
from jax import lax

D = 7168
TOKENS = 16384
VOCAB_WIN = 512
EMB_WIN = 64


def head_base(key):
    values = jax.random.normal(jax.random.fold_in(key, 11), (VOCAB_WIN, D), jnp.float32)
    return jnp.clip(values, -6.0, 6.0) * (12.0 / math.sqrt(D))


def draw_head(key, part):
    base = head_base(key)
    return jnp.clip(base, -1.0, 1.0).astype(jnp.bfloat16)


def draw_final_normed(key, part):
    key = jax.random.fold_in(key, 5)
    first_key = jax.random.fold_in(key, 0)
    values = jnp.clip(jax.random.normal(first_key, (TOKENS, D), jnp.float32), -6.0, 6.0) * 0.25
    return jnp.clip(values, -4.0, 4.0).astype(jnp.bfloat16)


def plant(array, key, smallest, high):
    longest = array.shape.index(max(array.shape))
    spots = []
    for shift in (0, 1):
        where = [jax.random.randint(jax.random.fold_in(key, axis), (), 0, length) for axis, length in enumerate(array.shape)]
        where[longest] = (where[longest] + shift) % array.shape[longest]
        spots.append(tuple(where))
    return array.at[spots[0]].set(smallest).at[spots[1]].set(high)


def level_of(stream_key, shape, pieces, least, top_value):
    loudness = 1.0
    for axis_at, shards_of in pieces:
        heights = jax.random.uniform(jax.random.fold_in(jax.random.fold_in(stream_key, 6), axis_at), (shards_of,), jnp.float32, least / len(pieces), top_value / len(pieces))
        loudness = loudness * jnp.repeat(jnp.exp(heights), shape[axis_at] // shards_of).reshape((-1,) + (1,) * (len(shape) - 1 - axis_at))
    return loudness


def cumulative_ranks(amount, lean):
    portions = [(1 << 20) // math.isqrt(rank ** lean) + 1 for rank in range(1, amount + 1)]
    scale = 1 + sum(portions) // (1 << 30)
    return np.cumsum(np.array([max(1, weight // scale) for weight in portions]))


def ranked(key, dims, count, slope):
    grid = cumulative_ranks(count, slope)
    ticket = jax.random.randint(jax.random.fold_in(key, 1), dims, 0, int(grid[count - 1]))
    rank = jnp.searchsorted(jnp.asarray(grid, jnp.int32), ticket, side="right")
    return jax.random.permutation(jax.random.fold_in(key, 2), count)[rank].astype(jnp.int32)


def bell_draw(own_key, extent, width, most, cuts=(), kind=jnp.bfloat16):
    array = width * jax.random.normal(own_key, extent, jnp.float32)
    if cuts:
        array = array * level_of(own_key, extent, cuts, -0.22, 0.18)
    return jnp.clip(array, -most, most).astype(kind)


def setup_inputs(seed: int = 0) -> dict:
    key_list = jax.random.split(jax.random.key(seed), 8)
    final_normed = draw_final_normed(jax.random.fold_in(key_list[7], 71), 0)
    embed_cot = bell_draw(key_list[1], (TOKENS, D), 0.3, 1.796875, ((0, 128), (1, 4)))
    head = draw_head(jax.random.fold_in(key_list[7], 71), 0)
    rest_lse = jnp.clip(6.0 + 6.0 * jax.random.uniform(key_list[3], (TOKENS,), jnp.float32) ** level_of(key_list[3], (TOKENS,), ((0, 128),), -0.2, 0.2), 6.0, 12.0)
    loss_grad = jnp.clip(jnp.exp(math.log(4.0) - 1.3862944 * jax.random.uniform(key_list[4], (TOKENS,), jnp.float32) ** level_of(key_list[4], (TOKENS,), ((0, 128),), -0.2, 0.2)), 1.0, 4.0)
    target_ids = plant(ranked(key_list[5], (TOKENS,), VOCAB_WIN, 1), jax.random.fold_in(key_list[5], 3), 0, VOCAB_WIN - 1).astype(jnp.int32)
    embed_ids = plant(ranked(key_list[6], (TOKENS,), EMB_WIN, 1), jax.random.fold_in(key_list[6], 3), 0, EMB_WIN - 1).astype(jnp.int32)
    return {"final_normed": final_normed, "embed_cot": embed_cot, "head": head, "rest_lse": rest_lse, "loss_grad": loss_grad, "target_ids": target_ids, "embed_ids": embed_ids}


def reference(final_normed, embed_cot, head, rest_lse, loss_grad, target_ids, embed_ids):
    logits = lax.dot_general(final_normed, head, (((1,), (1,)), ((), ())), preferred_element_type=jnp.float32)
    top = jnp.maximum(jnp.max(logits, axis=1), rest_lse)
    total = jnp.exp(rest_lse - top) + jnp.sum(jnp.exp(logits - top[:, None]), axis=1)
    log_total = top + jnp.log(total)
    columns = jnp.arange(VOCAB_WIN, dtype=jnp.int32)[None, :]
    target_hits = target_ids[:, None] == columns
    picked = jnp.sum(jnp.where(target_hits, logits, 0.0), axis=1)
    token_loss = log_total - picked
    dlogits = (loss_grad[:, None] * (jnp.exp(logits - log_total[:, None]) - target_hits.astype(jnp.float32))).astype(jnp.bfloat16)
    head_grad = lax.dot_general(dlogits, final_normed, (((0,), (0,)), ((), ())), preferred_element_type=jnp.float32)
    grad_hidden = jnp.dot(dlogits, head, preferred_element_type=jnp.float32).astype(jnp.bfloat16)
    onehot = (embed_ids[:, None] == jnp.arange(EMB_WIN, dtype=jnp.int32)[None, :]).astype(jnp.bfloat16)
    embed_grad = lax.dot_general(onehot, embed_cot, (((0,), (0,)), ((), ())), preferred_element_type=jnp.float32)
    return token_loss, grad_hidden, head_grad, embed_grad
```

```python
import jax
import jax.numpy as jnp
from jax import lax
from jax.sharding import Mesh
from jax.sharding import PartitionSpec as P

F32, BF16 = jnp.float32, jnp.bfloat16
RING = ("zhi", "tensor")
OWNERS = ("core", "tensor")
REPLICAS = ("x", "zhi", "core")


def dot(a, b, dims):
    return lax.dot_general(a, b, (dims, ((), ())), preferred_element_type=F32)


def shift(value, by):
    count = lax.axis_size(RING)
    return lax.ppermute(value, RING, [(i, (i + by) % count) for i in range(count)])


def swap_cores(value):
    return lax.ppermute(value, "core", [(0, 1), (1, 0)])


def exchange(value, axes):
    return lax.all_to_all(value, axes, 0, 0)


def spread(value, axes):
    count = lax.axis_size(axes)
    return exchange(jnp.broadcast_to(value[None], (count,) + value.shape), axes)


def window_quarter(head, core, rank, half):
    rows = head.shape[0]

    def block(ahead):
        at = (rank + ahead) % 4 * (2 * half) + core * half
        return lax.dynamic_slice_in_dim(head, at, half, 1)

    def row(ahead):
        return (rank + ahead) % 4 * rows

    after, before, across = block(1), block(3), block(2)
    middle = rows // 2
    pieces = (
        (shift(after, 1), row(3)),
        (shift(before, -1), row(1)),
        (shift(across[:middle], 2), row(2)),
        (shift(across[middle:], -2), row(2) + middle),
        (block(0), row(0)),
    )
    whole = jnp.zeros((4 * rows, half), head.dtype)
    for piece, at in pieces:
        whole = lax.dynamic_update_slice_in_dim(whole, piece, at, 0)
    return whole


def by_core(own, other, core):
    return jnp.where(core == 0, own, other), jnp.where(core == 0, other, own)


def three_parts(value):
    first = lax.reduce_precision(value, 8, 7)
    second = lax.reduce_precision(value - first, 8, 7)
    return first, second, value - first - second


def shards(final_normed, embed_cot, head, rest_lse, loss_grad, target_ids, embed_ids):
    core, rank = lax.axis_index("core"), lax.axis_index("tensor")
    tokens, width = final_normed.shape
    half = width // 2
    part = tokens // 4
    vocab = 4 * head.shape[0]
    replicas = lax.axis_size("dp")

    def own_half(value):
        return lax.dynamic_slice_in_dim(value, core * half, half, 1)

    def other_half(value):
        return lax.dynamic_slice_in_dim(value, (1 - core) * half, half, 1)

    window = window_quarter(head, core, rank, half)
    normed = jnp.concatenate(
        by_core(own_half(final_normed), swap_cores(other_half(final_normed)), core), 0
    )

    embed_rows = 8 * replicas
    onehot = (embed_ids[:, None] == lax.broadcasted_iota(jnp.int32, (1, embed_rows), 1)).astype(BF16)
    embed_term = dot(onehot, embed_cot, ((0,), (0,)))
    embed_term = own_half(embed_term) + swap_cores(other_half(embed_term).astype(BF16)).astype(F32)

    logits = dot(normed, window, ((1,), (1,)))
    logits = exchange(logits.reshape(8, part, vocab), OWNERS).sum(0)

    def own_part(value):
        return lax.dynamic_slice_in_dim(value, rank * part, part, 0)[:, None]

    lse_rest = own_part(rest_lse)
    hits = own_part(target_ids) == lax.broadcasted_iota(jnp.int32, (1, vocab), 1)
    top = jnp.maximum(jnp.max(logits, axis=1, keepdims=True), lse_rest)
    total = jnp.exp(lse_rest - top) + jnp.sum(jnp.exp(logits - top), axis=1, keepdims=True)
    lse = top + jnp.log(total)
    loss = lse - jnp.sum(jnp.where(hits, logits, 0.0), axis=1, keepdims=True)
    dlogits = own_part(loss_grad) * (jnp.exp(logits - lse) - hits.astype(F32))

    lane = lax.broadcasted_iota(jnp.int32, (part, 128), 1)
    first, second, third = three_parts(loss)
    extra = jnp.where(lane == 0, first, jnp.where(lane == 1, second, jnp.where(lane == 2, third, 0.0)))
    sent = jnp.concatenate((dlogits, extra), 1).astype(BF16)
    gathered = spread(sent, OWNERS).reshape(2 * tokens, vocab + 128)
    dlogits = gathered[:, :vocab]
    loss = lax.dynamic_slice_in_dim(gathered[:, vocab : vocab + 3], core * tokens, tokens, 0)
    token_loss = jnp.sum(loss.astype(F32), axis=1)

    head_term = dot(dlogits, normed, ((0,), (0,))).astype(BF16).reshape(4, vocab // 4, half)
    embed_term = (
        embed_term.astype(BF16).reshape(replicas, 4, 2, half).swapaxes(0, 1).reshape(4, 2 * replicas, half)
    )
    term = exchange(jnp.concatenate((head_term, embed_term), 1), "x").astype(F32).sum(0).astype(BF16)
    rows = vocab // 4 // replicas
    term = jnp.concatenate(
        (
            term[: vocab // 4].reshape(replicas, rows, half),
            term[vocab // 4 :].reshape(replicas, 2, half),
        ),
        1,
    )
    term = exchange(term, "dp").astype(F32).sum(0).astype(BF16)

    def owner(source):
        source, quarter = divmod(source, 4)
        source, at_core = divmod(source, 2)
        source, at_zhi = divmod(source, 2)
        at_dp, at_x = divmod(source, 4)
        return ((((2 * quarter + at_core) * 4 + at_dp // 2) * 2 + at_zhi) * 2 + at_dp % 2) * 4 + at_x

    every = ("dp",) + REPLICAS + ("tensor",)
    moved = lax.ppermute(term[:rows], every, [(i, owner(i)) for i in range(lax.axis_size(every))])
    pieces = spread(jnp.concatenate((moved, term[rows:]), 0), REPLICAS)
    pieces = pieces.astype(F32).reshape(4, 2, 2, rows + 2, half).sum(1)
    head_grad = pieces[:, :, :rows].reshape(vocab // 4, half)
    embed_grad = pieces[:, :, rows:].transpose(0, 2, 1, 3).reshape(8, width)

    grad_hidden = dot(dlogits, window, ((1,), (0,))).astype(BF16)
    mine = lax.dynamic_slice_in_dim(grad_hidden, core * tokens, tokens, 0)
    theirs = swap_cores(lax.dynamic_slice_in_dim(grad_hidden, (1 - core) * tokens, tokens, 0))
    grad_hidden = jnp.concatenate(by_core(mine, theirs, core), 1)
    return (token_loss, grad_hidden, head_grad, embed_grad)


def solution(mesh):
    sizes = (mesh.shape["dp"], 4, 2, 2, mesh.shape["tensor"])
    split = Mesh(mesh.devices.reshape(sizes), ("dp",) + REPLICAS + ("tensor",))
    token = ("dp",) + REPLICAS
    return jax.shard_map(
        shards,
        mesh=split,
        in_specs=(
            P(token, "tensor"),
            P(token, "tensor"),
            P("tensor", None),
            P(token),
            P(token),
            P(token),
            P(token),
        ),
        out_specs=(P(token), P(token, "tensor"), P("tensor", "dp"), P("dp", "tensor")),
        check_vma=False,
    )
```

```python
import jax
import jax.numpy as jnp
from jax import lax
from jax.sharding import Mesh
from jax.sharding import PartitionSpec as P

F32, BF16 = jnp.float32, jnp.bfloat16
RING = ("zhi", "tensor")
GROUP = ("x", "core")
EVERY = ("dp", "x", "zhi", "core", "tensor")
LANES = 128


def dot(a, b, dims):
    return lax.dot_general(a, b, (dims, ((), ())), preferred_element_type=F32)


def shift(value, by):
    count = lax.axis_size(RING)
    return lax.ppermute(value, RING, [(i, (i + by) % count) for i in range(count)])


def swap(value, axis):
    return lax.ppermute(value, axis, [(0, 1), (1, 0)])


def exchange(value, axes):
    return lax.all_to_all(value, axes, 0, 0)


def spread(value, axes):
    count = lax.axis_size(axes)
    return exchange(jnp.broadcast_to(value[None], (count,) + value.shape), axes)


def half_of(value, which):
    half = value.shape[1] // 2
    return lax.dynamic_slice_in_dim(value, which * half, half, 1)


def window_half(head, core, rank):
    rows, width = head.shape
    half = width // 8
    chunk = rows // 4

    def block(ahead):
        at = (rank + ahead) % 4 * (2 * half) + core * half
        return lax.dynamic_slice_in_dim(head, at, half, 1)

    across, middle = block(2), rows // 2
    pieces = (
        (shift(block(1), 1), 3, 0),
        (shift(block(3), -1), 1, 0),
        (shift(across[:middle], 2), 2, 0),
        (shift(across[middle:], -2), 2, 2),
        (block(0), 0, 0),
    )
    whole = jnp.zeros((4, 4, chunk, half), head.dtype)
    for piece, ahead, first in pieces:
        piece = piece.reshape(-1, 1, chunk, half)
        whole = lax.dynamic_update_slice(whole, piece, (first, (rank + ahead) % 4, 0, 0))
    return whole.reshape(4 * rows, half)


def three_parts(value):
    first = lax.reduce_precision(value, 8, 7)
    second = lax.reduce_precision(value - first, 8, 7)
    return first, second, value - first - second


def owner(flip):
    def place(source):
        source, quarter = divmod(source, 4)
        source, at_core = divmod(source, 2)
        source, at_zhi = divmod(source, 2)
        at_dp, at_x = divmod(source, 4)
        at_zhi = at_zhi ^ flip
        return ((((2 * quarter + at_core) * 4 + at_x) * 2 + at_zhi) * 2 + at_dp % 2) * 4 + at_dp // 2

    return [(i, place(i)) for i in range(lax.axis_size(EVERY))]


def shards(final_normed, embed_cot, head, rest_lse, loss_grad, target_ids, embed_ids):
    core, rank = lax.axis_index("core"), lax.axis_index("tensor")
    tokens, width = final_normed.shape
    half = width // 2
    part = tokens // 4
    vocab = 4 * head.shape[0]
    replicas = lax.axis_size("dp")

    mine = window_half(head, core, rank)
    other = swap(mine, "core")
    logits = dot(half_of(final_normed, core), mine, ((1,), (1,))) + dot(
        half_of(final_normed, 1 - core), other, ((1,), (1,))
    )
    logits = exchange(logits.reshape(4, part, vocab), "tensor").sum(0)

    halves = final_normed.reshape(tokens, 2, half).swapaxes(0, 1)
    normed = exchange(
        jnp.broadcast_to(halves[None], (4, 2, tokens, half)).reshape(8, tokens, half), GROUP
    ).reshape(8 * tokens, half)

    embed_rows = 8 * replicas
    onehot = (embed_ids[:, None] == lax.broadcasted_iota(jnp.int32, (1, embed_rows), 1)).astype(BF16)
    embed = dot(onehot, embed_cot, ((0,), (0,))).astype(BF16)
    embed = jnp.pad(embed, ((0, 0), (0, 16 * LANES - width)))
    embed = exchange(embed.reshape(embed_rows, 8, 2 * LANES).swapaxes(0, 1), GROUP).astype(F32).sum(0)
    embed = (embed + swap(embed.astype(BF16), "zhi").astype(F32)).astype(BF16)
    embed = jnp.concatenate(
        (
            embed[:, :LANES].reshape(replicas, 8, LANES),
            embed[:, LANES:].reshape(replicas, 8, LANES),
        ),
        1,
    )

    def own_part(value):
        return lax.dynamic_slice_in_dim(value, rank * part, part, 0)[:, None]

    lse_rest = own_part(rest_lse)
    column = lax.broadcasted_iota(jnp.int32, (1, vocab), 1)
    column = (column // 32 % 4) * 128 + column // 128 * 32 + column % 32
    hits = own_part(target_ids) == column
    top = jnp.maximum(jnp.max(logits, axis=1, keepdims=True), lse_rest)
    total = jnp.exp(lse_rest - top) + jnp.sum(jnp.exp(logits - top), axis=1, keepdims=True)
    lse = top + jnp.log(total)
    loss = lse - jnp.sum(jnp.where(hits, logits, 0.0), axis=1, keepdims=True)
    dlogits = own_part(loss_grad) * (jnp.exp(logits - lse) - hits.astype(F32))

    lane = lax.broadcasted_iota(jnp.int32, (part, LANES), 1)
    first, second, third = three_parts(loss)
    extra = jnp.where(lane == 0, first, jnp.where(lane == 1, second, jnp.where(lane == 2, third, 0.0)))
    sent = jnp.concatenate((dlogits, extra), 1).astype(BF16)
    gathered = spread(sent, "tensor").reshape(tokens, vocab + LANES)
    dlogits = gathered[:, :vocab]
    token_loss = jnp.sum(gathered[:, vocab : vocab + 3].astype(F32), axis=1)

    quarters = dlogits.reshape(tokens, 4, vocab // 4).swapaxes(0, 1)
    quarters = jnp.broadcast_to(quarters[:, None], (4, 2, tokens, vocab // 4))
    quarter = exchange(quarters.reshape(8, tokens, vocab // 4), GROUP).reshape(8 * tokens, vocab // 4)
    term = dot(quarter, normed, ((0,), (0,))).astype(BF16)
    term = jnp.concatenate((term.reshape(replicas, 16, half), embed), 2)
    term = exchange(term, "dp").astype(F32).sum(0).astype(BF16)

    block = term[:, :half]
    moved = lax.ppermute(block, EVERY, owner(0)).astype(F32) + lax.ppermute(
        block, EVERY, owner(1)
    ).astype(F32)
    pieces = spread(jnp.concatenate((moved.astype(BF16), term[:, half:]), 1), GROUP).astype(F32)
    head_grad = pieces[:, :, :half].reshape(vocab // 4, half)
    embed_grad = pieces[: width // (2 * LANES), :, half:].reshape(width // (2 * LANES), 2, 8, LANES)
    embed_grad = embed_grad.transpose(2, 0, 1, 3).reshape(8, width)

    out_mine = dot(dlogits, mine, ((1,), (0,))).astype(BF16)
    out_other = dot(dlogits, other, ((1,), (0,))).astype(BF16)
    grad_hidden = jnp.concatenate(
        (jnp.where(core == 0, out_mine, out_other), jnp.where(core == 0, out_other, out_mine)), 1
    )
    return (token_loss, grad_hidden, head_grad, embed_grad)


def solution(mesh):
    sizes = (mesh.shape["dp"], 4, 2, 2, mesh.shape["tensor"])
    split = Mesh(mesh.devices.reshape(sizes), EVERY)
    token = EVERY[:4]
    return jax.shard_map(
        shards,
        mesh=split,
        in_specs=(
            P(token, "tensor"),
            P(token, "tensor"),
            P("tensor", None),
            P(token),
            P(token),
            P(token),
            P(token),
        ),
        out_specs=(P(token), P(token, "tensor"), P("tensor", "dp"), P("dp", "tensor")),
        check_vma=False,
    )
```

```python
import jax
import jax.numpy as jnp
from jax import lax
from jax.sharding import Mesh
from jax.sharding import PartitionSpec as P

F32, BF16 = jnp.float32, jnp.bfloat16
RING = ("zhi", "tensor")
GROUP = ("x", "core")
EVERY = ("dp", "x", "zhi", "core", "tensor")
LANES = 128


def dot(a, b, dims):
    return lax.dot_general(a, b, (dims, ((), ())), preferred_element_type=F32)


def forward(at):
    return at + 1


def backward(at):
    return at - 1


def across(at):
    return at + 2 if at % 2 == 0 else at - 2


def shift(value, step):
    count = lax.axis_size(RING)
    return lax.ppermute(value, RING, [(i, step(i) % count) for i in range(count)])


def swap(value, axis):
    return lax.ppermute(value, axis, [(0, 1), (1, 0)])


def exchange(value, axes):
    return lax.all_to_all(value, axes, 0, 0)


def spread(value, axes):
    count = lax.axis_size(axes)
    return exchange(jnp.broadcast_to(value[None], (count,) + value.shape), axes)


def half_of(value, which):
    half = value.shape[1] // 2
    return lax.dynamic_slice_in_dim(value, which * half, half, 1)


def window_half(head, core, rank):
    rows, width = head.shape
    half = width // 8
    chunk = rows // 4

    def block(ahead):
        at = (rank + ahead) % 4 * (2 * half) + core * half
        return lax.dynamic_slice_in_dim(head, at, half, 1)

    pieces = (
        (shift(block(1), forward), 3),
        (shift(block(3), backward), 1),
        (shift(block(2), across), 2),
        (block(0), 0),
    )
    whole = jnp.zeros((4, 4, chunk, half), head.dtype)
    for piece, ahead in pieces:
        piece = piece.reshape(4, 1, chunk, half)
        whole = lax.dynamic_update_slice(whole, piece, (0, (rank + ahead) % 4, 0, 0))
    return whole.reshape(4 * rows, half)


def three_parts(value):
    first = lax.reduce_precision(value, 8, 7)
    second = lax.reduce_precision(value - first, 8, 7)
    return first, second, value - first - second


def owner(flip):
    def place(source):
        source, quarter = divmod(source, 4)
        source, at_core = divmod(source, 2)
        source, at_zhi = divmod(source, 2)
        at_dp, at_x = divmod(source, 4)
        at_zhi = at_zhi ^ flip
        return ((((2 * quarter + at_core) * 4 + at_x) * 2 + at_zhi) * 2 + at_dp % 2) * 4 + at_dp // 2

    return [(i, place(i)) for i in range(lax.axis_size(EVERY))]


def shards(final_normed, embed_cot, head, rest_lse, loss_grad, target_ids, embed_ids):
    core, rank = lax.axis_index("core"), lax.axis_index("tensor")
    tokens, width = final_normed.shape
    half = width // 2
    part = tokens // 4
    vocab = 4 * head.shape[0]
    replicas = lax.axis_size("dp")

    mine = window_half(head, core, rank)
    other = swap(mine, "core")
    logits = dot(half_of(final_normed, core), mine, ((1,), (1,))) + dot(
        half_of(final_normed, 1 - core), other, ((1,), (1,))
    )
    logits = exchange(logits.reshape(4, part, vocab), "tensor").sum(0)

    normed = lax.all_gather(final_normed, "x", axis=0, tiled=True)

    embed_rows = 8 * replicas
    onehot = (embed_ids[:, None] == lax.broadcasted_iota(jnp.int32, (1, embed_rows), 1)).astype(BF16)
    embed = dot(onehot, embed_cot, ((0,), (0,)))
    embed = jnp.pad(embed, ((0, 0), (0, 16 * LANES - width)))
    pairs = [embed[:, i * 4 * LANES : (i + 1) * 4 * LANES] for i in range(4)]
    embed = jnp.stack([half_of(pair, core) for pair in pairs])
    embed = embed + swap(jnp.stack([half_of(pair, 1 - core) for pair in pairs]), "core")
    embed = (embed + swap(embed.astype(BF16), "zhi").astype(F32)).astype(BF16)
    embed = jnp.concatenate((embed[:, :, :LANES], embed[:, :, LANES:]), 1)

    def own_part(value):
        return lax.dynamic_slice_in_dim(value, rank * part, part, 0)[:, None]

    lse_rest = own_part(rest_lse)
    column = lax.broadcasted_iota(jnp.int32, (1, vocab), 1)
    column = (column // 32 % 4) * 128 + column // 128 * 32 + column % 32
    hits = own_part(target_ids) == column
    top = jnp.maximum(jnp.max(logits, axis=1, keepdims=True), lse_rest)
    total = jnp.exp(lse_rest - top) + jnp.sum(jnp.exp(logits - top), axis=1, keepdims=True)
    lse = top + jnp.log(total)
    loss = lse - jnp.sum(jnp.where(hits, logits, 0.0), axis=1, keepdims=True)
    dlogits = own_part(loss_grad) * (jnp.exp(logits - lse) - hits.astype(F32))

    lane = lax.broadcasted_iota(jnp.int32, (part, LANES), 1)
    first, second, third = three_parts(loss)
    extra = jnp.where(lane == 0, first, jnp.where(lane == 1, second, jnp.where(lane == 2, third, 0.0)))
    sent = jnp.concatenate((dlogits, extra), 1).astype(BF16)
    gathered = spread(sent, "tensor").reshape(tokens, vocab + LANES)
    dlogits = gathered[:, :vocab]
    token_loss = jnp.sum(gathered[:, vocab : vocab + 3].astype(F32), axis=1)

    quarters = jnp.stack([dlogits[:, i * LANES : (i + 1) * LANES] for i in range(4)])
    quarters = exchange(jnp.concatenate((quarters, embed), 1), "x")
    term = dot(quarters[:, :tokens].reshape(4 * tokens, LANES), normed, ((0,), (0,)))
    embed = quarters[:, tokens:].astype(F32).sum(0).astype(BF16).reshape(2, replicas, 8, LANES)
    embed = jnp.concatenate((embed[0], embed[1]), 1)
    term = half_of(term, core) + swap(half_of(term, 1 - core).astype(BF16), "core").astype(F32)
    term = jnp.concatenate((term.astype(BF16).reshape(replicas, 16, half), embed), 2)
    term = exchange(term, "dp").astype(F32).sum(0).astype(BF16)

    block = term[:, :half]
    moved = lax.ppermute(block, EVERY, owner(0)).astype(F32) + lax.ppermute(
        block, EVERY, owner(1)
    ).astype(F32)
    pieces = spread(jnp.concatenate((moved.astype(BF16), term[:, half:]), 1), GROUP).astype(F32)
    head_grad = pieces[:, :, :half].reshape(vocab // 4, half)
    embed_grad = pieces[: width // (2 * LANES), :, half:].reshape(width // (2 * LANES), 2, 8, LANES)
    embed_grad = embed_grad.transpose(2, 0, 1, 3).reshape(8, width)

    out_mine = dot(dlogits, mine, ((1,), (0,))).astype(BF16)
    out_other = dot(dlogits, other, ((1,), (0,))).astype(BF16)
    grad_hidden = jnp.concatenate(
        (jnp.where(core == 0, out_mine, out_other), jnp.where(core == 0, out_other, out_mine)), 1
    )
    return (token_loss, grad_hidden, head_grad, embed_grad)


def solution(mesh):
    sizes = (mesh.shape["dp"], 4, 2, 2, mesh.shape["tensor"])
    split = Mesh(mesh.devices.reshape(sizes), EVERY)
    token = EVERY[:4]
    return jax.shard_map(
        shards,
        mesh=split,
        in_specs=(
            P(token, "tensor"),
            P(token, "tensor"),
            P("tensor", None),
            P(token),
            P(token),
            P(token),
            P(token),
        ),
        out_specs=(P(token), P(token, "tensor"), P("tensor", "dp"), P("dp", "tensor")),
        check_vma=False,
    )
```

```python
import jax
import jax.numpy as jnp
from jax import lax
from jax.sharding import Mesh
from jax.sharding import PartitionSpec as P

F32, BF16 = jnp.float32, jnp.bfloat16
RING = ("zhi", "tensor")
GROUP = ("x", "core")
EVERY = ("dp", "x", "zhi", "core", "tensor")
LANES = 128


def dot(a, b, dims):
    return lax.dot_general(a, b, (dims, ((), ())), preferred_element_type=F32)


def forward(at):
    return at + 1


def backward(at):
    return at - 1


def across(at):
    return at + 2 if at % 2 == 0 else at - 2


def shift(value, step):
    count = lax.axis_size(RING)
    return lax.ppermute(value, RING, [(i, step(i) % count) for i in range(count)])


def swap(value, axis):
    return lax.ppermute(value, axis, [(0, 1), (1, 0)])


def exchange(value, axes):
    return lax.all_to_all(value, axes, 0, 0)


def spread(value, axes):
    count = lax.axis_size(axes)
    return exchange(jnp.broadcast_to(value[None], (count,) + value.shape), axes)


def half_of(value, which):
    half = value.shape[1] // 2
    return lax.dynamic_slice_in_dim(value, which * half, half, 1)


def window_half(head, core, rank):
    rows, width = head.shape
    half = width // 8
    chunk = rows // 4

    def block(ahead):
        at = (rank + ahead) % 4 * (2 * half) + core * half
        return lax.dynamic_slice_in_dim(head, at, half, 1)

    pieces = (
        (shift(block(1), forward), 3),
        (shift(block(3), backward), 1),
        (shift(block(2), across), 2),
        (block(0), 0),
    )
    whole = jnp.zeros((4, 4, chunk, half), head.dtype)
    for piece, ahead in pieces:
        piece = piece.reshape(4, 1, chunk, half)
        whole = lax.dynamic_update_slice(whole, piece, (0, (rank + ahead) % 4, 0, 0))
    return whole.reshape(4 * rows, half)


def by_core(own, other, core):
    return jnp.concatenate((jnp.where(core == 0, own, other), jnp.where(core == 0, other, own)), 0)


def three_parts(value):
    first = lax.reduce_precision(value, 8, 7)
    second = lax.reduce_precision(value - first, 8, 7)
    return first, second, value - first - second


def owner(flip):
    def place(source):
        source, quarter = divmod(source, 4)
        source, at_core = divmod(source, 2)
        source, at_zhi = divmod(source, 2)
        at_dp, at_x = divmod(source, 4)
        at_zhi = at_zhi ^ flip
        return ((((2 * quarter + at_core) * 4 + at_x) * 2 + at_zhi) * 2 + at_dp % 2) * 4 + at_dp // 2

    return [(i, place(i)) for i in range(lax.axis_size(EVERY))]


def shards(final_normed, embed_cot, head, rest_lse, loss_grad, target_ids, embed_ids):
    core, rank = lax.axis_index("core"), lax.axis_index("tensor")
    tokens, width = final_normed.shape
    half = width // 2
    part = tokens // 4
    vocab = 4 * head.shape[0]
    replicas = lax.axis_size("dp")

    mine = window_half(head, core, rank)
    other = swap(mine, "core")
    logits = dot(half_of(final_normed, core), mine, ((1,), (1,))) + dot(
        half_of(final_normed, 1 - core), other, ((1,), (1,))
    )

    normed = swap(half_of(final_normed, 1 - core), "core")
    logits = exchange(logits.reshape(4, part, vocab), "tensor")
    logits, normed = lax.optimization_barrier((logits, normed))
    logits = logits.sum(0)
    normed = by_core(half_of(final_normed, core), normed, core)

    onehot = (embed_ids[:, None] == lax.broadcasted_iota(jnp.int32, (1, 8 * replicas), 1)).astype(BF16)
    embed = dot(onehot, embed_cot, ((0,), (0,)))
    embed = half_of(embed, core) + swap(half_of(embed, 1 - core), "core")
    embed = (embed + swap(embed.astype(BF16), "zhi").astype(F32)).astype(BF16)

    def own_part(value):
        return lax.dynamic_slice_in_dim(value, rank * part, part, 0)[:, None]

    lse_rest = own_part(rest_lse)
    column = lax.broadcasted_iota(jnp.int32, (1, vocab), 1)
    column = (column // 32 % 4) * 128 + column // 128 * 32 + column % 32
    hits = own_part(target_ids) == column
    top = jnp.maximum(jnp.max(logits, axis=1, keepdims=True), lse_rest)
    total = jnp.exp(lse_rest - top) + jnp.sum(jnp.exp(logits - top), axis=1, keepdims=True)
    lse = top + jnp.log(total)
    loss = lse - jnp.sum(jnp.where(hits, logits, 0.0), axis=1, keepdims=True)
    dlogits = own_part(loss_grad) * (jnp.exp(logits - lse) - hits.astype(F32))

    lane = lax.broadcasted_iota(jnp.int32, (part, LANES), 1)
    first, second, third = three_parts(loss)
    extra = jnp.where(lane == 0, first, jnp.where(lane == 1, second, jnp.where(lane == 2, third, 0.0)))
    sent = jnp.concatenate((dlogits, extra), 1).astype(BF16)

    gathered = spread(sent, "tensor").reshape(tokens, vocab + LANES)
    dlogits = gathered[:, :vocab]
    token_loss = jnp.sum(gathered[:, vocab : vocab + 3].astype(F32), axis=1)

    term = by_core(dlogits, swap(dlogits, "core"), core)
    term = dot(term, normed, ((0,), (0,))).astype(BF16).reshape(4, vocab // 4, half)
    term = exchange(term, "x").reshape(4, replicas, 16, half)
    embed = jnp.stack([embed.reshape(replicas, 8, half)] + [jnp.zeros((replicas, 8, half), BF16)] * 3)
    term = jnp.concatenate((term, embed), 2).astype(F32).sum(0).astype(BF16)
    term = exchange(term, "dp").astype(F32).sum(0).astype(BF16)

    block = term[:16]
    moved = lax.ppermute(block, EVERY, owner(0)).astype(F32) + lax.ppermute(
        block, EVERY, owner(1)
    ).astype(F32)
    pieces = spread(jnp.concatenate((moved.astype(BF16), term[16:]), 0), GROUP).astype(F32)
    head_grad = pieces[:, :16].reshape(vocab // 4, half)
    embed_grad = pieces[:, 16:].reshape(4, 2, 8, half).sum(0)
    embed_grad = jnp.concatenate((embed_grad[0], embed_grad[1]), 1)

    out_mine = dot(dlogits, mine, ((1,), (0,))).astype(BF16)
    out_other = dot(dlogits, other, ((1,), (0,))).astype(BF16)
    grad_hidden = jnp.concatenate(
        (jnp.where(core == 0, out_mine, out_other), jnp.where(core == 0, out_other, out_mine)), 1
    )
    return (token_loss, grad_hidden, head_grad, embed_grad)


def solution(mesh):
    sizes = (mesh.shape["dp"], 4, 2, 2, mesh.shape["tensor"])
    split = Mesh(mesh.devices.reshape(sizes), EVERY)
    token = EVERY[:4]
    return jax.shard_map(
        shards,
        mesh=split,
        in_specs=(
            P(token, "tensor"),
            P(token, "tensor"),
            P("tensor", None),
            P(token),
            P(token),
            P(token),
            P(token),
        ),
        out_specs=(P(token), P(token, "tensor"), P("tensor", "dp"), P("dp", "tensor")),
        check_vma=False,
    )
```

```python
import jax
import jax.numpy as jnp
from jax import lax
from jax.sharding import Mesh
from jax.sharding import PartitionSpec as P

F32, BF16 = jnp.float32, jnp.bfloat16
RING = ("zhi", "tensor")
GROUP = ("x", "core")
EVERY = ("dp", "x", "zhi", "core", "tensor")
LANES = 128


def dot(a, b, dims):
    return lax.dot_general(a, b, (dims, ((), ())), preferred_element_type=F32)


def forward(at):
    return at + 1


def backward(at):
    return at - 1


def across(at):
    return at + 2 if at % 2 == 0 else at - 2


def shift(value, step):
    count = lax.axis_size(RING)
    return lax.ppermute(value, RING, [(i, step(i) % count) for i in range(count)])


def swap(value, axis):
    return lax.ppermute(value, axis, [(0, 1), (1, 0)])


def exchange(value, axes):
    return lax.all_to_all(value, axes, 0, 0)


def spread(value, axes):
    count = lax.axis_size(axes)
    return exchange(jnp.broadcast_to(value[None], (count,) + value.shape), axes)


def half_of(value, which):
    half = value.shape[1] // 2
    return lax.dynamic_slice_in_dim(value, which * half, half, 1)


def window_half(head, core, rank):
    rows, width = head.shape
    half = width // 8
    chunk = rows // 4

    def block(ahead):
        at = (rank + ahead) % 4 * (2 * half) + core * half
        return lax.dynamic_slice_in_dim(head, at, half, 1)

    pieces = (
        (shift(block(1), forward), 3),
        (shift(block(3), backward), 1),
        (shift(block(2), across), 2),
        (block(0), 0),
    )
    whole = jnp.zeros((4, 4, chunk, half), head.dtype)
    for piece, ahead in pieces:
        piece = piece.reshape(4, 1, chunk, half)
        whole = lax.dynamic_update_slice(whole, piece, (0, (rank + ahead) % 4, 0, 0))
    return whole.reshape(4 * rows, half)


def by_core(own, other, core):
    return jnp.concatenate((jnp.where(core == 0, own, other), jnp.where(core == 0, other, own)), 0)


def three_parts(value):
    first = lax.reduce_precision(value, 8, 7)
    second = lax.reduce_precision(value - first, 8, 7)
    return first, second, value - first - second


def owner(flip):
    def place(source):
        source, quarter = divmod(source, 4)
        source, at_core = divmod(source, 2)
        source, at_zhi = divmod(source, 2)
        at_dp, at_x = divmod(source, 4)
        at_zhi = at_zhi ^ flip
        return ((((2 * quarter + at_core) * 4 + at_x) * 2 + at_zhi) * 2 + at_dp % 2) * 4 + at_dp // 2

    return [(i, place(i)) for i in range(lax.axis_size(EVERY))]


def shards(final_normed, embed_cot, head, rest_lse, loss_grad, target_ids, embed_ids):
    core, rank = lax.axis_index("core"), lax.axis_index("tensor")
    tokens, width = final_normed.shape
    half = width // 2
    part = tokens // 4
    vocab = 4 * head.shape[0]
    replicas = lax.axis_size("dp")

    mine = window_half(head, core, rank)
    other = swap(mine, "core")
    logits = dot(half_of(final_normed, core), mine, ((1,), (1,))) + dot(
        half_of(final_normed, 1 - core), other, ((1,), (1,))
    )

    onehot = (embed_ids[:, None] == lax.broadcasted_iota(jnp.int32, (1, 8 * replicas), 1)).astype(BF16)
    embed = dot(onehot, embed_cot, ((0,), (0,)))
    given = (half_of(final_normed, 1 - core), half_of(embed, 1 - core))
    logits, given = lax.optimization_barrier((logits, given))
    logits = exchange(logits.reshape(4, part, vocab), "tensor")
    taken = (swap(given[0], "core"), swap(given[1], "core"))
    logits, taken = lax.optimization_barrier((logits, taken))
    logits = logits.sum(0)
    normed = by_core(half_of(final_normed, core), taken[0], core)
    embed = half_of(embed, core) + taken[1]

    def own_part(value):
        pieces = [value[i * part : (i + 1) * part] for i in range(4)]
        low, high = (jnp.where(rank % 2 == 0, pieces[i], pieces[i + 1]) for i in (0, 2))
        return jnp.where(rank < 2, low, high)[:, None]

    lse_rest = own_part(rest_lse)
    column = lax.broadcasted_iota(jnp.int32, (1, vocab), 1)
    column = (column // 32 % 4) * 128 + column // 128 * 32 + column % 32
    hits = own_part(target_ids) == column
    top = jnp.maximum(jnp.max(logits, axis=1, keepdims=True), lse_rest)
    total = jnp.exp(lse_rest - top) + jnp.sum(jnp.exp(logits - top), axis=1, keepdims=True)
    lse = top + jnp.log(total)
    loss = lse - jnp.sum(jnp.where(hits, logits, 0.0), axis=1, keepdims=True)
    dlogits = own_part(loss_grad) * (jnp.exp(logits - lse) - hits.astype(F32))

    extra = jnp.concatenate(three_parts(loss) + (jnp.zeros((part, LANES - 3), F32),), 1)
    sent = jnp.concatenate((dlogits, extra), 1).astype(BF16)

    gathered = spread(sent, "tensor").reshape(tokens, vocab + LANES)
    dlogits = gathered[:, :vocab]
    token_loss = jnp.sum(gathered[:, vocab : vocab + 3].astype(F32), axis=1)

    term = by_core(dlogits, swap(dlogits, "core"), core)
    term = dot(term, normed, ((0,), (0,))).astype(BF16).reshape(4, vocab // 4, half)
    term = exchange(term, "x").reshape(4, replicas, 16, half)
    embed = (embed + swap(embed.astype(BF16), "zhi").astype(F32)).astype(BF16)
    embed = jnp.stack([embed.reshape(replicas, 8, half)] + [jnp.zeros((replicas, 8, half), BF16)] * 3)
    term = jnp.concatenate((term, embed), 2).astype(F32).sum(0).astype(BF16)
    term = exchange(term, "dp").astype(F32).sum(0).astype(BF16)

    block = term[:16]
    moved = lax.ppermute(block, EVERY, owner(0)).astype(F32) + lax.ppermute(
        block, EVERY, owner(1)
    ).astype(F32)
    pieces = spread(jnp.concatenate((moved.astype(BF16), term[16:]), 0), GROUP).astype(F32)
    head_grad = pieces[:, :16].reshape(vocab // 4, half)
    embed_grad = pieces[:, 16:].reshape(4, 2, 8, half).sum(0)
    embed_grad = jnp.concatenate((embed_grad[0], embed_grad[1]), 1)

    out_mine = dot(dlogits, mine, ((1,), (0,))).astype(BF16)
    out_other = dot(dlogits, other, ((1,), (0,))).astype(BF16)
    grad_hidden = jnp.concatenate(
        (jnp.where(core == 0, out_mine, out_other), jnp.where(core == 0, out_other, out_mine)), 1
    )
    return (token_loss, grad_hidden, head_grad, embed_grad)


def solution(mesh):
    sizes = (mesh.shape["dp"], 4, 2, 2, mesh.shape["tensor"])
    split = Mesh(mesh.devices.reshape(sizes), EVERY)
    token = EVERY[:4]
    return jax.shard_map(
        shards,
        mesh=split,
        in_specs=(
            P(token, "tensor"),
            P(token, "tensor"),
            P("tensor", None),
            P(token),
            P(token),
            P(token),
            P(token),
        ),
        out_specs=(P(token), P(token, "tensor"), P("tensor", "dp"), P("dp", "tensor")),
        check_vma=False,
    )
```

```python
import jax
import jax.numpy as jnp
from jax import lax
from jax.sharding import Mesh
from jax.sharding import PartitionSpec as P

F32, BF16 = jnp.float32, jnp.bfloat16
RING = ("zhi", "tensor")
GROUP = ("x", "core")
EVERY = ("dp", "x", "zhi", "core", "tensor")
LANES = 128


def dot(a, b, dims):
    return lax.dot_general(a, b, (dims, ((), ())), preferred_element_type=F32)


def forward(at):
    return at + 1


def backward(at):
    return at - 1


def across(at):
    return at + 2 if at % 2 == 0 else at - 2


def shift(value, step):
    count = lax.axis_size(RING)
    return lax.ppermute(value, RING, [(i, step(i) % count) for i in range(count)])


def swap(value, axis):
    return lax.ppermute(value, axis, [(0, 1), (1, 0)])


def exchange(value, axes):
    return lax.all_to_all(value, axes, 0, 0)


def spread(value, axes):
    count = lax.axis_size(axes)
    return exchange(jnp.broadcast_to(value[None], (count,) + value.shape), axes)


def half_of(value, which):
    half = value.shape[1] // 2
    return lax.dynamic_slice_in_dim(value, which * half, half, 1)


def window_half(head, core, rank):
    rows, width = head.shape
    half = width // 8
    chunk = rows // 4

    def block(ahead):
        at = (rank + ahead) % 4 * (2 * half) + core * half
        return lax.dynamic_slice_in_dim(head, at, half, 1)

    pieces = (
        (shift(block(1), forward), 3),
        (shift(block(3), backward), 1),
        (shift(block(2), across), 2),
        (block(0), 0),
    )
    whole = jnp.zeros((4, 4, chunk, half), head.dtype)
    for piece, ahead in pieces:
        piece = piece.reshape(4, 1, chunk, half)
        whole = lax.dynamic_update_slice(whole, piece, (0, (rank + ahead) % 4, 0, 0))
    return whole.reshape(4 * rows, half)


def by_core(own, other, core):
    return jnp.concatenate((jnp.where(core == 0, own, other), jnp.where(core == 0, other, own)), 0)


def three_parts(value):
    first = lax.reduce_precision(value, 8, 7)
    second = lax.reduce_precision(value - first, 8, 7)
    return first, second, value - first - second


def owner(flip):
    def place(source):
        source, quarter = divmod(source, 4)
        source, at_core = divmod(source, 2)
        source, at_zhi = divmod(source, 2)
        at_dp, at_x = divmod(source, 4)
        at_zhi = at_zhi ^ flip
        return ((((2 * quarter + at_core) * 4 + at_x) * 2 + at_zhi) * 2 + at_dp % 2) * 4 + at_dp // 2

    return [(i, place(i)) for i in range(lax.axis_size(EVERY))]


def shards(final_normed, embed_cot, head, rest_lse, loss_grad, target_ids, embed_ids):
    core, rank = lax.axis_index("core"), lax.axis_index("tensor")
    tokens, width = final_normed.shape
    half = width // 2
    part = tokens // 4
    vocab = 4 * head.shape[0]
    replicas = lax.axis_size("dp")

    onehot = (embed_ids[:, None] == lax.broadcasted_iota(jnp.int32, (1, 8 * replicas), 1)).astype(BF16)
    embed = dot(onehot, embed_cot, ((0,), (0,)))
    taken = (swap(half_of(final_normed, 1 - core), "core"), swap(half_of(embed, 1 - core), "core"))

    mine = window_half(head, core, rank)
    mine, taken = lax.optimization_barrier((mine, taken))
    other = swap(mine, "core")
    logits = dot(half_of(final_normed, core), mine, ((1,), (1,))) + dot(
        half_of(final_normed, 1 - core), other, ((1,), (1,))
    )
    normed = by_core(half_of(final_normed, core), taken[0], core)
    embed = half_of(embed, core) + taken[1]

    def from_x(value, ahead):
        return lax.ppermute(value, "x", [((i + ahead) % 4, i) for i in range(4)])

    far = from_x(normed, 2)
    logits, own = lax.optimization_barrier((logits, normed))
    logits = exchange(logits.reshape(4, part, vocab), "tensor")
    after, before = from_x(own, 1), from_x(own, 3)
    logits, far = lax.optimization_barrier((logits, far))
    logits = logits.sum(0)

    def own_part(value):
        pieces = [value[i * part : (i + 1) * part] for i in range(4)]
        low, high = (jnp.where(rank % 2 == 0, pieces[i], pieces[i + 1]) for i in (0, 2))
        return jnp.where(rank < 2, low, high)[:, None]

    lse_rest = own_part(rest_lse)
    column = lax.broadcasted_iota(jnp.int32, (1, vocab), 1)
    column = (column // 32 % 4) * 128 + column // 128 * 32 + column % 32
    hits = own_part(target_ids) == column
    top = jnp.maximum(jnp.max(logits, axis=1, keepdims=True), lse_rest)
    total = jnp.exp(lse_rest - top) + jnp.sum(jnp.exp(logits - top), axis=1, keepdims=True)
    lse = top + jnp.log(total)
    loss = lse - jnp.sum(jnp.where(hits, logits, 0.0), axis=1, keepdims=True)
    dlogits = own_part(loss_grad) * (jnp.exp(logits - lse) - hits.astype(F32))

    extra = jnp.concatenate(three_parts(loss) + (jnp.zeros((part, LANES - 3), F32),), 1)
    sent = jnp.concatenate((dlogits, extra), 1).astype(BF16)

    quarters = jnp.stack([sent[:, i * LANES : (i + 1) * LANES] for i in range(4)])
    quarters = jnp.broadcast_to(quarters[:, None], (4, 8, part, LANES)).reshape(32, part, LANES)
    def joined(value, step):
        other = lax.ppermute(value, "tensor", [(i, i ^ step) for i in range(4)])
        first = (rank & step) == 0
        return jnp.concatenate((jnp.where(first, value, other), jnp.where(first, other, value)), 0)

    quarters, sent = lax.optimization_barrier((quarters, sent))
    quarter = exchange(quarters, GROUP + ("tensor",)).reshape(4, 2 * tokens, LANES)
    sent = joined(sent, 1)
    normed = jnp.concatenate((own, after, far, before), 0)
    quarter, normed, sent = lax.optimization_barrier((quarter, normed, sent))
    quarter = lax.dynamic_slice_in_dim(jnp.concatenate((quarter, quarter[:3]), 0), lax.axis_index("x"), 4, 0)
    term = dot(quarter.reshape(8 * tokens, LANES), normed, ((0,), (0,))).astype(BF16)
    embed = embed.astype(BF16)
    term = jnp.concatenate((term.reshape(replicas, 16, half), embed.reshape(replicas, 8, half)), 1)
    term, sent = lax.optimization_barrier((term, sent))
    term = exchange(term, "dp")
    gathered = joined(sent, 2)
    term, gathered = lax.optimization_barrier((term, gathered))
    term = term.astype(F32).sum(0)
    dlogits = gathered[:, :vocab]
    token_loss = jnp.sum(gathered[:, vocab : vocab + 3].astype(F32), axis=1)

    block, embed = term[:16].astype(BF16), term[16:]
    moved = lax.ppermute(block, EVERY, owner(0)).astype(F32) + lax.ppermute(
        block, EVERY, owner(1)
    ).astype(F32)
    embed = embed + swap(embed.astype(BF16), "zhi").astype(F32)
    pieces = spread(jnp.concatenate((moved, embed), 0).astype(BF16), GROUP).astype(F32)
    head_grad = pieces[:, :16].reshape(vocab // 4, half)
    embed_grad = pieces[:, 16:].reshape(4, 2, 8, half).sum(0)
    embed_grad = jnp.concatenate((embed_grad[0], embed_grad[1]), 1)

    out_mine = dot(dlogits, mine, ((1,), (0,))).astype(BF16)
    out_other = dot(dlogits, other, ((1,), (0,))).astype(BF16)
    grad_hidden = jnp.concatenate(
        (jnp.where(core == 0, out_mine, out_other), jnp.where(core == 0, out_other, out_mine)), 1
    )
    return (token_loss, grad_hidden, head_grad, embed_grad)


def solution(mesh):
    sizes = (mesh.shape["dp"], 4, 2, 2, mesh.shape["tensor"])
    split = Mesh(mesh.devices.reshape(sizes), EVERY)
    token = EVERY[:4]
    return jax.shard_map(
        shards,
        mesh=split,
        in_specs=(
            P(token, "tensor"),
            P(token, "tensor"),
            P("tensor", None),
            P(token),
            P(token),
            P(token),
            P(token),
        ),
        out_specs=(P(token), P(token, "tensor"), P("tensor", "dp"), P("dp", "tensor")),
        check_vma=False,
    )
```

```python
import jax
import jax.numpy as jnp
from jax import lax
from jax.sharding import Mesh
from jax.sharding import PartitionSpec as P

F32, BF16 = jnp.float32, jnp.bfloat16
RING = ("zhi", "tensor")
GROUP = ("x", "core")
EVERY = ("dp", "x", "zhi", "core", "tensor")
LANES = 128


def dot(a, b, dims):
    return lax.dot_general(a, b, (dims, ((), ())), preferred_element_type=F32)


def forward(at):
    return at + 1


def backward(at):
    return at - 1


def across(at):
    return at + 2 if at % 2 == 0 else at - 2


def shift(value, step):
    count = lax.axis_size(RING)
    return lax.ppermute(value, RING, [(i, step(i) % count) for i in range(count)])


def swap(value, axis):
    return lax.ppermute(value, axis, [(0, 1), (1, 0)])


def exchange(value, axes):
    return lax.all_to_all(value, axes, 0, 0)


def spread(value, axes):
    count = lax.axis_size(axes)
    return exchange(jnp.broadcast_to(value[None], (count,) + value.shape), axes)


def half_of(value, which):
    half = value.shape[1] // 2
    return lax.dynamic_slice_in_dim(value, which * half, half, 1)


def window_half(head, core, rank):
    rows, width = head.shape
    half = width // 8
    chunk = rows // 4

    def block(ahead):
        at = (rank + ahead) % 4 * (2 * half) + core * half
        return lax.dynamic_slice_in_dim(head, at, half, 1)

    pieces = (
        (shift(block(1), forward), 3),
        (shift(block(3), backward), 1),
        (shift(block(2), across), 2),
        (block(0), 0),
    )
    whole = jnp.zeros((4, 4, chunk, half), head.dtype)
    for piece, ahead in pieces:
        piece = piece.reshape(4, 1, chunk, half)
        whole = lax.dynamic_update_slice(whole, piece, (0, (rank + ahead) % 4, 0, 0))
    return whole.reshape(4 * rows, half)


def three_parts(value):
    first = lax.reduce_precision(value, 8, 7)
    second = lax.reduce_precision(value - first, 8, 7)
    return first, second, value - first - second


def owner():
    def place(source):
        source, quarter = divmod(source, 4)
        source, at_core = divmod(source, 2)
        source, at_zhi = divmod(source, 2)
        at_dp, at_x = divmod(source, 4)
        return ((((2 * quarter + at_core) * 4 + at_x) * 2 + at_zhi) * 2 + at_dp % 2) * 4 + at_dp // 2

    return [(i, place(i)) for i in range(lax.axis_size(EVERY))]


def shards(final_normed, embed_cot, head, rest_lse, loss_grad, target_ids, embed_ids):
    core, rank = lax.axis_index("core"), lax.axis_index("tensor")
    tokens, width = final_normed.shape
    half = width // 2
    part = tokens // 4
    vocab = 4 * head.shape[0]
    replicas = lax.axis_size("dp")

    onehot = (embed_ids[:, None] == lax.broadcasted_iota(jnp.int32, (1, 8 * replicas), 1)).astype(BF16)
    embed = dot(onehot, embed_cot, ((0,), (0,))).astype(BF16)
    normed = jnp.concatenate(
        (half_of(final_normed, core), swap(half_of(final_normed, 1 - core), "core")), 0
    )
    taken = swap(half_of(embed, 1 - core), "core")

    mine = window_half(head, core, rank)
    mine, normed, taken = lax.optimization_barrier((mine, normed, taken))
    other = swap(mine, "core")
    logits = dot(half_of(final_normed, core), mine, ((1,), (1,))) + dot(
        half_of(final_normed, 1 - core), other, ((1,), (1,))
    )

    def from_x(value, ahead):
        return lax.ppermute(value, "x", [((i + ahead) % 4, i) for i in range(4)])

    far = from_x(normed, 2)
    logits, own = lax.optimization_barrier((logits, normed))
    logits = exchange(logits.reshape(4, part, vocab), "tensor")
    after, before = from_x(own, 1), from_x(own, 3)
    logits, far = lax.optimization_barrier((logits, far))
    logits = logits.sum(0)

    def own_part(value):
        pieces = [value[i * part : (i + 1) * part] for i in range(4)]
        low, high = (jnp.where(rank % 2 == 0, pieces[i], pieces[i + 1]) for i in (0, 2))
        return jnp.where(rank < 2, low, high)[:, None]

    lse_rest = own_part(rest_lse)
    column = lax.broadcasted_iota(jnp.int32, (1, vocab), 1)
    column = (column // 32 % 4) * 128 + column // 128 * 32 + column % 32
    hits = own_part(target_ids) == column
    top = jnp.maximum(jnp.max(logits, axis=1, keepdims=True), lse_rest)
    total = jnp.exp(lse_rest - top) + jnp.sum(jnp.exp(logits - top), axis=1, keepdims=True)
    lse = top + jnp.log(total)
    loss = lse - jnp.sum(jnp.where(hits, logits, 0.0), axis=1, keepdims=True)
    dlogits = own_part(loss_grad) * (jnp.exp(logits - lse) - hits.astype(F32))

    extra = jnp.concatenate(three_parts(loss) + (jnp.zeros((part, LANES - 3), F32),), 1)
    sent = jnp.concatenate((dlogits, extra), 1).astype(BF16)

    quarters = jnp.stack([sent[:, i * LANES : (i + 1) * LANES] for i in range(4)])
    quarters = jnp.broadcast_to(quarters[:, None], (4, 8, part, LANES)).reshape(32, part, LANES)
    def joined(value, other, step):
        first = (rank & step) == 0
        return jnp.concatenate((jnp.where(first, value, other), jnp.where(first, other, value)), 0)

    def partner(value, step):
        return lax.ppermute(value, "tensor", [(i, i ^ step) for i in range(4)])

    quarters, sent, taken = lax.optimization_barrier((quarters, sent, taken))
    quarter = exchange(quarters, GROUP + ("tensor",)).reshape(4, 2 * tokens, LANES)
    pair = partner(sent, 1)
    normed = jnp.concatenate((own, after, far, before), 0)
    pair, normed = lax.optimization_barrier((pair, normed))
    sent = joined(sent, pair, 1)
    quarter, normed, sent = lax.optimization_barrier((quarter, normed, sent))
    quarter = lax.dynamic_slice_in_dim(jnp.concatenate((quarter, quarter[:3]), 0), lax.axis_index("x"), 4, 0)
    turned = jnp.concatenate((quarter[:, tokens:], quarter[:, :tokens]), 1)
    quarter = jnp.where(core == 0, quarter, turned)
    term = dot(quarter.reshape(8 * tokens, LANES), normed, ((0,), (0,))).astype(BF16)
    embed = (half_of(embed, core).astype(F32) + taken.astype(F32)).astype(BF16)
    term = jnp.concatenate((term.reshape(replicas, 16, half), embed.reshape(replicas, 8, half)), 1)
    term, sent = lax.optimization_barrier((term, sent))
    term = exchange(term, "dp")
    pair = partner(sent, 2)
    term, pair = lax.optimization_barrier((term, pair))
    gathered = joined(sent, pair, 2)
    term = term.astype(F32).sum(0)
    dlogits = gathered[:, :vocab]
    token_loss = jnp.sum(gathered[:, vocab : vocab + 3].astype(F32), axis=1)

    term = (term + swap(term.astype(BF16), "zhi").astype(F32)).astype(BF16)
    block = lax.ppermute(term[:16], EVERY, owner())
    pieces = spread(jnp.concatenate((block, term[16:]), 0), GROUP).astype(F32)
    head_grad = pieces[:, :16].reshape(vocab // 4, half)
    embed_grad = pieces[:, 16:].reshape(4, 2, 8, half).sum(0)
    embed_grad = jnp.concatenate((embed_grad[0], embed_grad[1]), 1)

    out_mine = dot(dlogits, mine, ((1,), (0,))).astype(BF16)
    out_other = dot(dlogits, other, ((1,), (0,))).astype(BF16)
    grad_hidden = jnp.concatenate(
        (jnp.where(core == 0, out_mine, out_other), jnp.where(core == 0, out_other, out_mine)), 1
    )
    return (token_loss, grad_hidden, head_grad, embed_grad)


def solution(mesh):
    sizes = (mesh.shape["dp"], 4, 2, 2, mesh.shape["tensor"])
    split = Mesh(mesh.devices.reshape(sizes), EVERY)
    token = EVERY[:4]
    return jax.shard_map(
        shards,
        mesh=split,
        in_specs=(
            P(token, "tensor"),
            P(token, "tensor"),
            P("tensor", None),
            P(token),
            P(token),
            P(token),
            P(token),
        ),
        out_specs=(P(token), P(token, "tensor"), P("tensor", "dp"), P("dp", "tensor")),
        check_vma=False,
    )
```

```python
import jax
import jax.numpy as jnp
from jax import lax
from jax.sharding import Mesh
from jax.sharding import PartitionSpec as P

F32, BF16 = jnp.float32, jnp.bfloat16
RING = ("zhi", "tensor")
GROUP = ("x", "core")
EVERY = ("dp", "x", "zhi", "core", "tensor")
LANES = 128


def dot(a, b, dims):
    return lax.dot_general(a, b, (dims, ((), ())), preferred_element_type=F32)


def forward(at):
    return at + 1


def backward(at):
    return at - 1


def across(at):
    return at + 2 if at % 2 == 0 else at - 2


def shift(value, step):
    count = lax.axis_size(RING)
    return lax.ppermute(value, RING, [(i, step(i) % count) for i in range(count)])


def swap(value, axis):
    return lax.ppermute(value, axis, [(0, 1), (1, 0)])


def exchange(value, axes):
    return lax.all_to_all(value, axes, 0, 0)


def spread(value, axes):
    count = lax.axis_size(axes)
    return exchange(jnp.broadcast_to(value[None], (count,) + value.shape), axes)


def half_of(value, which):
    half = value.shape[1] // 2
    return lax.dynamic_slice_in_dim(value, which * half, half, 1)


def window_half(head, core, rank):
    rows, width = head.shape
    half = width // 8
    chunk = rows // 8

    def block(ahead):
        at = (rank + ahead) % 4 * (2 * half) + core * half
        return lax.dynamic_slice_in_dim(head, at, half, 1)

    pieces = (
        (shift(block(1), forward), 3),
        (shift(block(3), backward), 1),
        (shift(block(2), across), 2),
        (block(0), 0),
    )
    whole = jnp.zeros((4, 2, 4, chunk, half), head.dtype)
    for piece, ahead in pieces:
        piece = piece.reshape(4, 2, 1, chunk, half)
        whole = lax.dynamic_update_slice(whole, piece, (0, 0, (rank + ahead) % 4, 0, 0))
    return whole.reshape(4 * rows, half)


def three_parts(value):
    first = lax.reduce_precision(value, 8, 7)
    second = lax.reduce_precision(value - first, 8, 7)
    return first, second, value - first - second


def owner():
    def place(source):
        source, quarter = divmod(source, 4)
        source, at_core = divmod(source, 2)
        source, at_zhi = divmod(source, 2)
        at_dp, at_x = divmod(source, 4)
        return ((((2 * quarter + at_core) * 4 + at_x) * 2 + at_zhi) * 2 + at_dp // 4) * 4 + at_dp % 4

    return [(i, place(i)) for i in range(lax.axis_size(EVERY))]


def shards(final_normed, embed_cot, head, rest_lse, loss_grad, target_ids, embed_ids):
    core, rank = lax.axis_index("core"), lax.axis_index("tensor")
    tokens, width = final_normed.shape
    half = width // 2
    part = tokens // 4
    vocab = 4 * head.shape[0]
    replicas = lax.axis_size("dp")

    onehot = (embed_ids[:, None] == lax.broadcasted_iota(jnp.int32, (1, 8 * replicas), 1)).astype(BF16)
    embed = dot(onehot, embed_cot, ((0,), (0,))).astype(BF16)
    normed = jnp.concatenate(
        (half_of(final_normed, core), swap(half_of(final_normed, 1 - core), "core")), 0
    )
    taken = swap(half_of(embed, 1 - core), "core")

    mine = window_half(head, core, rank)
    mine, normed, taken = lax.optimization_barrier((mine, normed, taken))
    other = swap(mine, "core")
    logits = dot(half_of(final_normed, core), mine, ((1,), (1,))) + dot(
        half_of(final_normed, 1 - core), other, ((1,), (1,))
    )

    def from_x(value, ahead):
        return lax.ppermute(value, "x", [((i + ahead) % 4, i) for i in range(4)])

    far = from_x(normed, 2)
    logits, own = lax.optimization_barrier((logits, normed))
    logits = exchange(logits.reshape(4, part, vocab), "tensor")
    after, before = from_x(own, 1), from_x(own, 3)
    logits, far = lax.optimization_barrier((logits, far))
    logits = logits.sum(0)

    def own_part(value):
        pieces = [value[i * part : (i + 1) * part] for i in range(4)]
        low, high = (jnp.where(rank % 2 == 0, pieces[i], pieces[i + 1]) for i in (0, 2))
        return jnp.where(rank < 2, low, high)[:, None]

    lse_rest = own_part(rest_lse)
    column = lax.broadcasted_iota(jnp.int32, (1, vocab), 1)
    column = column // 16 % 4 * 128 + column // 64 * 16 + column % 16
    hits = own_part(target_ids) == column
    top = jnp.maximum(jnp.max(logits, axis=1, keepdims=True), lse_rest)
    total = jnp.exp(lse_rest - top) + jnp.sum(jnp.exp(logits - top), axis=1, keepdims=True)
    lse = top + jnp.log(total)
    loss = lse - jnp.sum(jnp.where(hits, logits, 0.0), axis=1, keepdims=True)
    dlogits = own_part(loss_grad) * (jnp.exp(logits - lse) - hits.astype(F32))

    extra = jnp.concatenate(three_parts(loss) + (jnp.zeros((part, LANES - 3), F32),), 1)
    sent = jnp.concatenate((dlogits, extra), 1).astype(BF16)

    quarters = jnp.stack([sent[:, i * LANES : (i + 1) * LANES] for i in range(4)])
    quarters = jnp.broadcast_to(quarters[:, None], (4, 8, part, LANES)).reshape(32, part, LANES)
    def joined(value, other, step):
        first = (rank & step) == 0
        return jnp.concatenate((jnp.where(first, value, other), jnp.where(first, other, value)), 0)

    def partner(value, step):
        return lax.ppermute(value, "tensor", [(i, i ^ step) for i in range(4)])

    quarters, sent, taken = lax.optimization_barrier((quarters, sent, taken))
    quarter = exchange(quarters, GROUP + ("tensor",)).reshape(4, 2 * tokens, LANES)
    pair = partner(sent, 1)
    normed = jnp.concatenate((own, after, far, before), 0)
    pair, normed = lax.optimization_barrier((pair, normed))
    sent = joined(sent, pair, 1)
    quarter, normed, sent = lax.optimization_barrier((quarter, normed, sent))
    quarter = lax.dynamic_slice_in_dim(jnp.concatenate((quarter, quarter[:3]), 0), lax.axis_index("x"), 4, 0)
    turned = jnp.concatenate((quarter[:, tokens:], quarter[:, :tokens]), 1)
    quarter = jnp.where(core == 0, quarter, turned)
    term = dot(quarter.reshape(8 * tokens, LANES), normed, ((0,), (0,))).astype(BF16)
    embed = (half_of(embed, core).astype(F32) + taken.astype(F32)).astype(BF16)
    term = jnp.concatenate((term.reshape(replicas, 16, half), embed.reshape(replicas, 8, half)), 1)
    term, sent = lax.optimization_barrier((term, sent))
    term = exchange(term, "dp")
    pair = partner(sent, 2)
    term, pair = lax.optimization_barrier((term, pair))
    gathered = joined(sent, pair, 2)
    term = term.astype(F32).sum(0)
    dlogits = gathered[:, :vocab]
    token_loss = jnp.sum(gathered[:, vocab : vocab + 3].astype(F32), axis=1)

    term = (term + swap(term.astype(BF16), "zhi").astype(F32)).astype(BF16)
    block = lax.ppermute(term[:16], EVERY, owner())
    pieces = spread(jnp.concatenate((block, term[16:]), 0), GROUP).astype(F32)
    head_grad = pieces[:, :16].reshape(vocab // 4, half)
    embed_grad = pieces[:, 16:].reshape(4, 2, 8, half).sum(0)
    embed_grad = jnp.concatenate((embed_grad[0], embed_grad[1]), 1)

    out_mine = dot(dlogits, mine, ((1,), (0,))).astype(BF16)
    out_other = dot(dlogits, other, ((1,), (0,))).astype(BF16)
    grad_hidden = jnp.concatenate(
        (jnp.where(core == 0, out_mine, out_other), jnp.where(core == 0, out_other, out_mine)), 1
    )
    return (token_loss, grad_hidden, head_grad, embed_grad)


def solution(mesh):
    sizes = (mesh.shape["dp"], 4, 2, 2, mesh.shape["tensor"])
    split = Mesh(mesh.devices.reshape(sizes), EVERY)
    token = EVERY[:4]
    return jax.shard_map(
        shards,
        mesh=split,
        in_specs=(
            P(token, "tensor"),
            P(token, "tensor"),
            P("tensor", None),
            P(token),
            P(token),
            P(token),
            P(token),
        ),
        out_specs=(P(token), P(token, "tensor"), P("tensor", "dp"), P("dp", "tensor")),
        check_vma=False,
    )
```

```python
import jax
import jax.numpy as jnp
from jax import lax
from jax.sharding import Mesh
from jax.sharding import PartitionSpec as P

F32, BF16 = jnp.float32, jnp.bfloat16
RING = ("zhi", "tensor")
GROUP = ("x", "core")
EVERY = ("dp", "x", "zhi", "core", "tensor")
LANES = 128


def dot(a, b, dims):
    return lax.dot_general(a, b, (dims, ((), ())), preferred_element_type=F32)


def forward(at):
    return at + 1


def backward(at):
    return at - 1


def across(at):
    return at + 2 if at % 2 == 0 else at - 2


def shift(value, step):
    count = lax.axis_size(RING)
    return lax.ppermute(value, RING, [(i, step(i) % count) for i in range(count)])


def swap(value, axis):
    return lax.ppermute(value, axis, [(0, 1), (1, 0)])


def exchange(value, axes):
    return lax.all_to_all(value, axes, 0, 0)


def spread(value, axes):
    count = lax.axis_size(axes)
    return exchange(jnp.broadcast_to(value[None], (count,) + value.shape), axes)


def half_of(value, which):
    half = value.shape[1] // 2
    return lax.dynamic_slice_in_dim(value, which * half, half, 1)


def window_half(head, core, rank):
    rows, width = head.shape
    half = width // 8
    chunk = rows // 8

    def block(ahead):
        at = (rank + ahead) % 4 * (2 * half) + core * half
        return lax.dynamic_slice_in_dim(head, at, half, 1)

    pieces = (
        (shift(block(1), forward), 3),
        (shift(block(3), backward), 1),
        (shift(block(2), across), 2),
        (block(0), 0),
    )
    whole = jnp.zeros((4, 2, 4, chunk, half), head.dtype)
    for piece, ahead in pieces:
        piece = piece.reshape(4, 2, 1, chunk, half)
        whole = lax.dynamic_update_slice(whole, piece, (0, 0, (rank + ahead) % 4, 0, 0))
    return whole.reshape(4 * rows, half)


def three_parts(value):
    first = lax.reduce_precision(value, 8, 7)
    second = lax.reduce_precision(value - first, 8, 7)
    return first, second, value - first - second


def owner():
    def place(source):
        source, quarter = divmod(source, 4)
        source, at_core = divmod(source, 2)
        source, at_zhi = divmod(source, 2)
        at_dp, at_x = divmod(source, 4)
        return ((((2 * quarter + at_core) * 4 + at_x) * 2 + at_zhi) * 2 + at_dp // 4) * 4 + at_dp % 4

    return [(i, place(i)) for i in range(lax.axis_size(EVERY))]


def shards(final_normed, embed_cot, head, rest_lse, loss_grad, target_ids, embed_ids):
    core, rank = lax.axis_index("core"), lax.axis_index("tensor")
    tokens, width = final_normed.shape
    half = width // 2
    part = tokens // 4
    vocab = 4 * head.shape[0]
    replicas = lax.axis_size("dp")

    onehot = (embed_ids[:, None] == lax.broadcasted_iota(jnp.int32, (1, 8 * replicas), 1)).astype(BF16)
    embed = dot(onehot, embed_cot, ((0,), (0,))).astype(BF16)
    normed = jnp.concatenate(
        (half_of(final_normed, core), swap(half_of(final_normed, 1 - core), "core")), 0
    )
    taken = swap(half_of(embed, 1 - core), "core")

    mine = window_half(head, core, rank)
    mine, normed, taken = lax.optimization_barrier((mine, normed, taken))
    other = swap(mine, "core")
    logits = dot(half_of(final_normed, core), mine, ((1,), (1,))) + dot(
        half_of(final_normed, 1 - core), other, ((1,), (1,))
    )

    def from_x(value, ahead):
        return lax.ppermute(value, "x", [((i + ahead) % 4, i) for i in range(4)])

    far = from_x(normed, 2)
    logits, own = lax.optimization_barrier((logits, normed))
    logits = exchange(logits.reshape(4, part, vocab), "tensor")
    after, before = from_x(own, 1), from_x(own, 3)
    logits, far = lax.optimization_barrier((logits, far))
    logits = logits.sum(0)

    def own_part(value):
        pieces = [value[i * part : (i + 1) * part] for i in range(4)]
        low, high = (jnp.where(rank % 2 == 0, pieces[i], pieces[i + 1]) for i in (0, 2))
        return jnp.where(rank < 2, low, high)[:, None]

    lse_rest = own_part(rest_lse)
    column = lax.broadcasted_iota(jnp.int32, (1, vocab), 1)
    column = column // 16 % 4 * 128 + column // 64 * 16 + column % 16
    hits = own_part(target_ids) == column
    top = jnp.maximum(jnp.max(logits, axis=1, keepdims=True), lse_rest)
    total = jnp.exp(lse_rest - top) + jnp.sum(jnp.exp(logits - top), axis=1, keepdims=True)
    lse = top + jnp.log(total)
    loss = lse - jnp.sum(jnp.where(hits, logits, 0.0), axis=1, keepdims=True)
    dlogits = own_part(loss_grad) * (jnp.exp(logits - lse) - hits.astype(F32))

    extra = jnp.concatenate(three_parts(loss) + (jnp.zeros((part, LANES - 3), F32),), 1)
    sent = jnp.concatenate((dlogits, extra), 1).astype(BF16)

    quarters = jnp.stack([sent[:, i * LANES : (i + 1) * LANES] for i in range(4)])
    quarters = jnp.broadcast_to(quarters[:, None], (4, 8, part, LANES)).reshape(32, part, LANES)
    def joined(value, other, step):
        first = (rank & step) == 0
        return jnp.concatenate((jnp.where(first, value, other), jnp.where(first, other, value)), 0)

    def partner(value, step):
        return lax.ppermute(value, "tensor", [(i, i ^ step) for i in range(4)])

    quarters, sent, taken = lax.optimization_barrier((quarters, sent, taken))
    quarter = exchange(quarters, GROUP + ("tensor",)).reshape(4, 2 * tokens, LANES)
    pair = partner(sent, 1)
    normed = jnp.concatenate((own, after, far, before), 0)
    embed = (half_of(embed, core).astype(F32) + taken.astype(F32)).astype(BF16)
    pair, normed, embed = lax.optimization_barrier((pair, normed, embed))
    sent = joined(sent, pair, 1)
    quarter, normed, sent = lax.optimization_barrier((quarter, normed, sent))
    quarter = lax.dynamic_slice_in_dim(jnp.concatenate((quarter, quarter[:3]), 0), lax.axis_index("x"), 4, 0)
    turned = jnp.concatenate((quarter[:, tokens:], quarter[:, :tokens]), 1)
    quarter = jnp.where(core == 0, quarter, turned)
    term = dot(quarter.reshape(8 * tokens, LANES), normed, ((0,), (0,))).astype(BF16)
    term = jnp.concatenate((term.reshape(replicas, 16, half), embed.reshape(replicas, 8, half)), 1)
    term, sent = lax.optimization_barrier((term, sent))
    term = exchange(term, "dp")
    pair = partner(sent, 2)
    term, pair = lax.optimization_barrier((term, pair))
    gathered = joined(sent, pair, 2)
    term = term.astype(F32).sum(0)
    dlogits = gathered[:, :vocab]
    token_loss = jnp.sum(gathered[:, vocab : vocab + 3].astype(F32), axis=1)

    term = (term + swap(term.astype(BF16), "zhi").astype(F32)).astype(BF16)
    block = lax.ppermute(term[:16], EVERY, owner())
    pieces = spread(jnp.concatenate((block, term[16:]), 0), GROUP).astype(F32)
    head_grad = pieces[:, :16].reshape(vocab // 4, half)
    embed_grad = pieces[:, 16:].reshape(4, 2, 8, half).sum(0)
    embed_grad = jnp.concatenate((embed_grad[0], embed_grad[1]), 1)

    out_mine = dot(dlogits, mine, ((1,), (0,))).astype(BF16)
    out_other = dot(dlogits, other, ((1,), (0,))).astype(BF16)
    grad_hidden = jnp.concatenate(
        (jnp.where(core == 0, out_mine, out_other), jnp.where(core == 0, out_other, out_mine)), 1
    )
    return (token_loss, grad_hidden, head_grad, embed_grad)


def solution(mesh):
    sizes = (mesh.shape["dp"], 4, 2, 2, mesh.shape["tensor"])
    split = Mesh(mesh.devices.reshape(sizes), EVERY)
    token = EVERY[:4]
    return jax.shard_map(
        shards,
        mesh=split,
        in_specs=(
            P(token, "tensor"),
            P(token, "tensor"),
            P("tensor", None),
            P(token),
            P(token),
            P(token),
            P(token),
        ),
        out_specs=(P(token), P(token, "tensor"), P("tensor", "dp"), P("dp", "tensor")),
        check_vma=False,
    )
```
